32 devices in a mesh: batch: 2 (over x), blk: 16 (over z, y, core).
Axes of the slice: x: 2, y: 2, z: 4, core: 2. Of those that a mesh axis runs over, the one named last changes fastest.
Arguments:
- ids: int32 [4, 1024], P('batch', 'blk'), may hold values from 0 to 31
- targets: int32 [4, 1024], P('batch', 'blk'), may hold values from 0 to 31
- flags: int32 [4, 1024], P('batch', 'blk'), may hold values from 0 to 1
- tags: int32 [4], replicated, may hold values from 1 to 4
- partner: int32 [4], replicated, may hold values from 0 to 3, as said below
- embedding: float32 [32, 1024], P(None, 'blk'), may hold values from -4 to 4
- gains: float32 [2, 1024], P(None, 'blk')
- attn_qkv: float32 [1024, 3072], P('blk'), may hold values from -0.1875 to 0.1875
- attn_out: float32 [1024, 1024], P('blk'), may hold values from -3 to 3
- mlp_in: float32 [1024, 4096], P('blk'), may hold values from -0.1875 to 0.1875
- mlp_out: float32 [4096, 1024], P('blk'), may hold values from -0.09375 to 0.09375
- out_head: float32 [1024, 32], P('blk'), may hold values from -0.1875 to 0.1875
- first_embedding: float32 [32, 1024], P(None, 'blk'), may hold values from -9.536743e-07 to 9.536743e-07
- first_gains: float32 [2, 1024], P(None, 'blk'), may hold values from -9.536743e-07 to 9.536743e-07
- first_attn_qkv: float32 [1024, 3072], P('blk'), may hold values from -9.536743e-07 to 9.536743e-07
- first_attn_out: float32 [1024, 1024], P('blk'), may hold values from -9.536743e-07 to 9.536743e-07
- first_mlp_in: float32 [1024, 4096], P('blk'), may hold values from -9.536743e-07 to 9.536743e-07
- first_mlp_out: float32 [4096, 1024], P('blk'), may hold values from -9.536743e-07 to 9.536743e-07
- first_out_head: float32 [1024, 32], P('blk'), may hold values from -9.536743e-07 to 9.536743e-07
- second_embedding: float32 [32, 1024], P(None, 'blk'), may hold values from 1.976207e-15 to 7.904828e-15
- second_gains: float32 [2, 1024], P(None, 'blk'), may hold values from 1.976207e-15 to 7.904828e-15
- second_attn_qkv: float32 [1024, 3072], P('blk'), may hold values from 1.976207e-15 to 7.904828e-15
- second_attn_out: float32 [1024, 1024], P('blk'), may hold values from 9.881036e-17 to 3.9524143e-16
- second_mlp_in: float32 [1024, 4096], P('blk'), may hold values from 6.5610074e-17 to 2.6085933e-16
- second_mlp_out: float32 [4096, 1024], P('blk'), may hold values from 2.4504968e-16 to 9.881035e-16
- second_out_head: float32 [1024, 32], P('blk'), may hold values from 1.976207e-15 to 7.904828e-15
Outputs:
- loss_terms: float32 [2], replicated
- pair_loss: float32 [], replicated
- grad_norm: float32 [], replicated
- new_embedding: float32 [32, 1024], P(None, 'blk')
- moment_one_embedding: float32 [32, 1024], P(None, 'blk')
- moment_two_embedding: float32 [32, 1024], P(None, 'blk')
- new_gains: float32 [2, 1024], P(None, 'blk')
- moment_one_gains: float32 [2, 1024], P(None, 'blk')
- moment_two_gains: float32 [2, 1024], P(None, 'blk')
- new_attn_qkv: float32 [1024, 3072], P('blk')
- moment_one_attn_qkv: float32 [1024, 3072], P('blk')
- moment_two_attn_qkv: float32 [1024, 3072], P('blk')
- new_attn_out: float32 [1024, 1024], P('blk')
- moment_one_attn_out: float32 [1024, 1024], P('blk')
- moment_two_attn_out: float32 [1024, 1024], P('blk')
- new_mlp_in: float32 [1024, 4096], P('blk')
- moment_one_mlp_in: float32 [1024, 4096], P('blk')
- moment_two_mlp_in: float32 [1024, 4096], P('blk')
- new_mlp_out: float32 [4096, 1024], P('blk')
- moment_one_mlp_out: float32 [4096, 1024], P('blk')
- moment_two_mlp_out: float32 [4096, 1024], P('blk')
- new_out_head: float32 [1024, 32], P('blk')
- moment_one_out_head: float32 [1024, 32], P('blk')
- moment_two_out_head: float32 [1024, 32], P('blk')
The draws below stay inside these ranges and needn't reach their ends.
Inputs may be any that keep to these rules, and one draw needn't show every extreme that they name: partner[partner[s]] = s and partner[s] != s for every sequence s.
All inputs are finite; a program needn't handle non-finite values.
Results may differ from the reference program's by a relative error of at most 0.024.
Values may be sent and summed in bfloat16 or wider, within the bound.
No kernel may reach another device: no remote copies, remote signals or barrier semaphores. Data moves between devices by JAX's collectives and lax.ppermute only.
A program may use at most 320 MiB of HBM per device.

```python
import math
import jax
import jax.numpy as jnp
from jax import lax

D = 1024
FF = 4096
H = 16
HD = 64
ROT = 32
VOCAB = 32
ADAM_STEP = 10
LENGTH = 1024
NSEQ = 4
NPARAM = 12650496


def draw_gains(key, part):
    key = jax.random.fold_in(key, 11)
    ramp = jnp.arange(D).astype(jnp.float32) / D
    noise = jax.random.normal(key, (2, D), jnp.float32)
    return (0.5 + ramp)[None, :] * (1.0 + 0.1 * jnp.clip(noise, -4.0, 4.0))


def draw_flags(key, part):
    key = jax.random.fold_in(key, 12)
    position = jnp.arange(LENGTH, dtype=jnp.int32)
    upper = (jnp.arange(NSEQ, dtype=jnp.int32) >= NSEQ // 2).astype(jnp.int32)
    level = (250 + 600 * position // LENGTH)[None, :] * (4 + 6 * upper)[:, None] // 10
    return (jax.random.randint(key, (NSEQ, LENGTH), 0, 1000) < level).astype(jnp.int32)


def draw_partner(key, part):
    key = jax.random.fold_in(key, 13)
    order = jax.random.permutation(key, NSEQ).astype(jnp.int32)
    swapped = order.reshape(NSEQ // 2, 2)[:, ::-1].reshape(NSEQ)
    return jnp.zeros((NSEQ,), jnp.int32).at[order].set(swapped)


def with_ends(values, key, smallest, high):
    extent = values.shape
    place = [jax.random.randint(jax.random.fold_in(key, axis), (), 0, extent[axis]) for axis in range(len(extent))]
    values = values.at[tuple(place)].set(smallest)
    longest = extent.index(max(extent))
    place[longest] = (place[longest] + 1) % extent[longest]
    return values.at[tuple(place)].set(high)


def block_levels(key, shape, cuts, smallest, high):
    gain, own = 1.0, jax.random.fold_in(key, 6)
    for axis_at, shards_of in cuts:
        heights = jnp.exp(jax.random.uniform(jax.random.fold_in(own, axis_at), (shards_of,), jnp.float32, smallest / len(cuts), high / len(cuts)))
        gain = gain * jnp.repeat(heights, shape[axis_at] // shards_of).reshape([-1 if axis == axis_at else 1 for axis in range(len(shape))])
    return gain


def gaussian(key, extent, width, most, split=(), held_as=jnp.bfloat16):
    values = jax.random.normal(key, extent, jnp.float32) * width
    if len(split) > 0:
        values = block_levels(key, extent, split, -0.22, 0.18) * values
    return jnp.clip(values, min=-most, max=most).astype(held_as)


def setup_inputs(seed: int = 0) -> dict:
    arg_keys = jax.random.split(jax.random.key(seed), 27)
    return {
        "ids": with_ends(jax.random.randint(arg_keys[0], (NSEQ, LENGTH), 0, VOCAB), jax.random.fold_in(arg_keys[0], 1), 0, VOCAB - 1).astype(jnp.int32),
        "targets": with_ends(jax.random.randint(arg_keys[1], (NSEQ, LENGTH), 0, VOCAB), jax.random.fold_in(arg_keys[1], 1), 0, VOCAB - 1).astype(jnp.int32),
        "flags": draw_flags(jax.random.fold_in(arg_keys[26], 71), 0),
        "tags": with_ends(jax.random.randint(arg_keys[3], (NSEQ,), 1, 5), jax.random.fold_in(arg_keys[3], 1), 1, 4).astype(jnp.int32),
        "partner": draw_partner(jax.random.fold_in(arg_keys[26], 71), 0),
        "embedding": gaussian(arg_keys[5], (VOCAB, D), 1.0, 4.0, ((1, 16),), jnp.float32),
        "gains": draw_gains(jax.random.fold_in(arg_keys[26], 71), 0),
        "attn_qkv": gaussian(arg_keys[7], (D, 3 * D), D ** -0.5, 0.1875, ((0, 16),), jnp.float32),
        "attn_out": gaussian(arg_keys[8], (D, D), (D // 256) ** -0.5, 3.0, ((0, 16),), jnp.float32),
        "mlp_in": gaussian(arg_keys[9], (D, FF), D ** -0.5, 0.1875, ((0, 16),), jnp.float32),
        "mlp_out": gaussian(arg_keys[10], (FF, D), FF ** -0.5, 0.09375, ((0, 16),), jnp.float32),
        "out_head": gaussian(arg_keys[11], (D, VOCAB), D ** -0.5, 0.1875, ((0, 16),), jnp.float32),
        "first_embedding": gaussian(arg_keys[12], (VOCAB, D), (0.00055 * NPARAM ** -0.5), 9.5367431640625e-07, ((1, 16),), jnp.float32),
        "first_gains": gaussian(arg_keys[13], (2, D), (0.00055 * NPARAM ** -0.5), 9.5367431640625e-07, ((1, 16),), jnp.float32),
        "first_attn_qkv": gaussian(arg_keys[14], (D, 3 * D), (0.00055 * NPARAM ** -0.5), 9.5367431640625e-07, ((0, 16),), jnp.float32),
        "first_attn_out": gaussian(arg_keys[15], (D, D), (0.00055 * NPARAM ** -0.5), 9.5367431640625e-07, ((0, 16),), jnp.float32),
        "first_mlp_in": gaussian(arg_keys[16], (D, FF), (0.00055 * NPARAM ** -0.5), 9.5367431640625e-07, ((0, 16),), jnp.float32),
        "first_mlp_out": gaussian(arg_keys[17], (FF, D), (0.00055 * NPARAM ** -0.5), 9.5367431640625e-07, ((0, 16),), jnp.float32),
        "first_out_head": gaussian(arg_keys[18], (D, VOCAB), (0.00055 * NPARAM ** -0.5), 9.5367431640625e-07, ((0, 16),), jnp.float32),
        "second_embedding": jnp.clip(jnp.exp(math.log(7.904828254099404e-15) - 1.3862944 * jax.random.uniform(arg_keys[19], (VOCAB, D), jnp.float32) ** block_levels(arg_keys[19], (VOCAB, D), ((1, 16),), -0.2, 0.2)), 1.976207063524851e-15, 7.904828254099404e-15),
        "second_gains": jnp.clip(jnp.exp(math.log(7.904828254099404e-15) - 1.3862944 * jax.random.uniform(arg_keys[20], (2, D), jnp.float32) ** block_levels(arg_keys[20], (2, D), ((1, 16),), -0.2, 0.2)), 1.976207063524851e-15, 7.904828254099404e-15),
        "second_attn_qkv": jnp.clip(jnp.exp(math.log(7.904828254099404e-15) - 1.3862944 * jax.random.uniform(arg_keys[21], (D, 3 * D), jnp.float32) ** block_levels(arg_keys[21], (D, 3 * D), ((0, 16),), -0.2, 0.2)), 1.976207063524851e-15, 7.904828254099404e-15),
        "second_attn_out": jnp.clip(jnp.exp(math.log(3.9524142858683795e-16) - 1.3862944 * jax.random.uniform(arg_keys[22], (D, D), jnp.float32) ** block_levels(arg_keys[22], (D, D), ((0, 16),), -0.2, 0.2)), 9.881035714670949e-17, 3.9524142858683795e-16),
        "second_mlp_in": jnp.clip(jnp.exp(math.log(2.60859333867588e-16) - 1.3802521 * jax.random.uniform(arg_keys[23], (D, FF), jnp.float32) ** block_levels(arg_keys[23], (D, FF), ((0, 16),), -0.2, 0.2)), 6.561007359846463e-17, 2.60859333867588e-16),
        "second_mlp_out": jnp.clip(jnp.exp(math.log(9.881035317624255e-16) - 1.39432653 * jax.random.uniform(arg_keys[24], (FF, D), jnp.float32) ** block_levels(arg_keys[24], (FF, D), ((0, 16),), -0.2, 0.2)), 2.450496756653233e-16, 9.881035317624255e-16),
        "second_out_head": jnp.clip(jnp.exp(math.log(7.904828254099404e-15) - 1.3862944 * jax.random.uniform(arg_keys[25], (D, VOCAB), jnp.float32) ** block_levels(arg_keys[25], (D, VOCAB), ((0, 16),), -0.2, 0.2)), 1.976207063524851e-15, 7.904828254099404e-15),
    }


@jax.custom_vjp
def low(v):
    return lax.optimization_barrier(v.astype(jnp.bfloat16)).astype(jnp.float32)

@jax.custom_vjp
def low_back(v):
    return v

def low_keep(v):
    return (low(v), None)

def low_pass(kept, grad):
    return (grad,)

def back_keep(v):
    return (v, None)

def back_low(kept, grad):
    return (low(grad),)
low.defvjp(low_keep, low_pass)
low_back.defvjp(back_keep, back_low)
norm_eps = 1e-05
z_weight = 0.02
pair_weight = 4.0
clip_level = 0.005
beta_one = 0.9
beta_two = 0.999
adam_eps = 1e-08
weight_decay = 0.1
learn_rates = (0.5, 0.5, 0.02, 0.2, 0.02, 0.01, 0.02)
decay_flags = (0.0, 0.0, 1.0, 1.0, 1.0, 1.0, 1.0)
masked_value = -1e+30

def matmul(left, right):
    return jnp.dot(left, right, precision=lax.Precision.HIGHEST)

def normalize(stream, gain_row):
    average = lax.optimization_barrier(jnp.mean(stream, -1, keepdims=True))
    centered = stream - average
    variance = lax.optimization_barrier(jnp.mean(centered * centered, -1, keepdims=True))
    return centered * lax.rsqrt(variance + norm_eps) * gain_row

def rotate(values, position):
    half_rot = ROT // 2
    frequency = jnp.exp(jnp.arange(half_rot).astype(jnp.float32) * (-2.0 * math.log(10000.0) / ROT))
    angles = position[:, None] * frequency[None, :]
    cosine = jnp.cos(angles)[:, None, :]
    sine_part = jnp.sin(angles)[:, None, :]
    leading = values[..., :half_rot]
    trailing = values[..., half_rot:ROT]
    return jnp.concatenate([leading * cosine - trailing * sine_part, trailing * cosine + leading * sine_part, values[..., ROT:]], -1)

def adam_update(weight, moment_one, moment_two, gradient, rate, decay_flag):
    moment_one = beta_one * moment_one + (1.0 - beta_one) * gradient
    moment_two = beta_two * moment_two + (1.0 - beta_two) * gradient * gradient
    stepped = moment_one / (1.0 - beta_one ** ADAM_STEP) / (jnp.sqrt(moment_two / (1.0 - beta_two ** ADAM_STEP)) + adam_eps)
    return (weight - rate * (stepped + weight_decay * decay_flag * weight), moment_one, moment_two)

def attend_block(first_row, queries, key_rows, values):
    scores = low_back(jnp.einsum('qhd,khd->hqk', queries, key_rows, precision=lax.Precision.HIGHEST))
    allowed = jnp.arange(key_rows.shape[0])[None, :] <= (first_row + jnp.arange(queries.shape[0]))[:, None]
    log_total = jax.nn.logsumexp(jnp.where(allowed, scores, masked_value), -1, keepdims=True)
    attn_prob = low(jnp.where(allowed, jnp.exp(scores - log_total), 0.0))
    return jnp.einsum('hqk,khd->qhd', attn_prob, values, precision=lax.Precision.HIGHEST)

def sequence_stats(lowered, tokens, goal_ids, counted):
    embed_table, gain_pair, w_qkv, w_attn, w_inner, w_outer, w_head = lowered
    length = tokens.shape[0]
    stream = embed_table[tokens]
    normed = low(normalize(stream, gain_pair[0]))
    projected = low_back(matmul(normed, w_qkv)).reshape(length, 3, H, HD)
    position = jnp.arange(length).astype(jnp.float32)
    queries = low(rotate(projected[:, 0], position) * HD ** (-0.5))
    key_rows = low(rotate(projected[:, 1], position))
    values = low(projected[:, 2])
    block_rows = min(512, length)
    block_starts = jnp.arange(0, length, block_rows).astype(jnp.int32)
    query_blocks = queries.reshape(length // block_rows, block_rows, H, HD)
    blockwise = jax.checkpoint(attend_block)
    attended = lax.map(lambda element: blockwise(element[0], element[1], key_rows, values), (block_starts, query_blocks))
    attended = low_back(low(attended.reshape(length, H * HD)))
    inner = low_back(matmul(normed, w_inner))
    activated = low(jax.nn.gelu(inner, approximate=True))
    branch = low_back(matmul(attended, w_attn) + matmul(activated, w_outer))
    mixed = stream + branch
    final = low(normalize(mixed, gain_pair[1]))
    logits = low_back(matmul(final, w_head))
    log_total = jax.nn.logsumexp(logits, -1)
    picked = jnp.take_along_axis(logits, goal_ids[:, None], -1)[:, 0] - log_total
    weight_rows = counted.astype(jnp.float32)
    return (jnp.sum(weight_rows * picked), jnp.sum(weight_rows), jnp.sum(weight_rows * log_total * log_total))

def reference(ids, targets, flags, tags, partner, embedding, gains, attn_qkv, attn_out, mlp_in, mlp_out, out_head, first_embedding, first_gains, first_attn_qkv, first_attn_out, first_mlp_in, first_mlp_out, first_out_head, second_embedding, second_gains, second_attn_qkv, second_attn_out, second_mlp_in, second_mlp_out, second_out_head):
    masters = (embedding, gains, attn_qkv, attn_out, mlp_in, mlp_out, out_head)
    firsts = (first_embedding, first_gains, first_attn_qkv, first_attn_out, first_mlp_in, first_mlp_out, first_out_head)
    seconds = (second_embedding, second_gains, second_attn_qkv, second_attn_out, second_mlp_in, second_mlp_out, second_out_head)

    def total_loss(params):
        lowered = tuple((low(weight) for weight in params))
        per_sequence = jax.checkpoint(sequence_stats)
        stats = lax.map(lambda element: per_sequence(lowered, element[0], element[1], element[2]), (ids, targets, flags))
        seq_ll, seq_count, seq_square = stats
        token_count = jnp.sum(seq_count)
        pair_gap = (seq_ll - seq_ll[partner]) / LENGTH
        pair_term = pair_weight / NSEQ * jnp.sum(tags.astype(jnp.float32) * pair_gap * pair_gap)
        head_term = -jnp.sum(seq_ll) + z_weight * jnp.sum(seq_square)
        return (head_term / token_count + pair_term, (jnp.stack([head_term, token_count]), pair_term))
    loss_value, pullback, aux_terms = jax.vjp(total_loss, masters, has_aux=True)
    loss_terms, pair_loss = aux_terms
    gradients = pullback(jnp.ones((), jnp.float32))[0]
    grad_norm = jnp.sqrt(sum((jnp.sum(gradient * gradient) for gradient in gradients)))
    clip_scale = clip_level / jnp.maximum(grad_norm, clip_level)
    updated = [adam_update(masters[member], firsts[member], seconds[member], gradients[member] * clip_scale, learn_rates[member], decay_flags[member]) for member in range(7)]
    return (loss_terms, pair_loss, grad_norm, updated[0][0], updated[0][1], updated[0][2], updated[1][0], updated[1][1], updated[1][2], updated[2][0], updated[2][1], updated[2][2], updated[3][0], updated[3][1], updated[3][2], updated[4][0], updated[4][1], updated[4][2], updated[5][0], updated[5][1], updated[5][2], updated[6][0], updated[6][1], updated[6][2])
```

```python
import math

import jax
import jax.numpy as jnp
from jax import lax
from jax.experimental import pallas as pl
from jax.experimental.pallas import tpu as pltpu
from jax.sharding import PartitionSpec as P

H = 16
HD = 64
ROT = 32
VOCAB = 32
ADAM_STEP = 10
GROUP = 4

norm_eps = 1e-05
z_weight = 0.02
pair_weight = 4.0
clip_level = 0.005
beta_one = 0.9
beta_two = 0.999
adam_eps = 1e-08
weight_decay = 0.1
learn_rates = (0.5, 0.5, 0.02, 0.2, 0.02, 0.01, 0.02)
decay_flags = (0.0, 0.0, 1.0, 1.0, 1.0, 1.0, 1.0)
masked_value = -1e30
f32 = jnp.float32
bf16 = jnp.bfloat16
both = ("batch", "blk")
VMEM_BYTES = 60 * 1024 * 1024


def dot(left, right):
    return jnp.dot(left, right, preferred_element_type=f32)


def dot_nt(left, right):
    return lax.dot_general(left, right, (((1,), (1,)), ((), ())), preferred_element_type=f32)


def dot_tn(left, right):
    return lax.dot_general(left, right, (((0,), (0,)), ((), ())), preferred_element_type=f32)


def low(values):
    return lax.reduce_precision(values, 8, 7)


def split(values, count):
    pieces = []
    for _ in range(count):
        piece = low(values)
        pieces.append(piece.astype(bf16))
        values = values - piece
    return pieces


def adam_update(weight, moment_one, moment_two, gradient, rate, decay_flag):
    moment_one = beta_one * moment_one + (1.0 - beta_one) * gradient
    moment_two = beta_two * moment_two + (1.0 - beta_two) * gradient * gradient
    stepped = (
        moment_one
        / (1.0 - beta_one**ADAM_STEP)
        / (jnp.sqrt(moment_two / (1.0 - beta_two**ADAM_STEP)) + adam_eps)
    )
    return (weight - rate * (stepped + weight_decay * decay_flag * weight), moment_one, moment_two)


def swap_pairs(values):
    width = values.shape[1]
    lane = lax.broadcasted_iota(jnp.int32, values.shape, 1) % HD
    from_right = pltpu.roll(values, width - ROT // 2, 1)
    from_left = pltpu.roll(values, ROT // 2, 1)
    return jnp.where(lane < ROT // 2, -from_right, jnp.where(lane < ROT, from_left, 0.0))


def own_head(seg):
    shape = (GROUP * seg, GROUP * HD)
    return (
        lax.broadcasted_iota(jnp.int32, shape, 0) // seg
        == lax.broadcasted_iota(jnp.int32, shape, 1) // HD
    )


def spread_heads(rows, seg):
    return jnp.where(own_head(seg), jnp.concatenate([rows] * GROUP, 0), 0.0)


def pick_heads(square, seg):
    lane_head = lax.broadcasted_iota(jnp.int32, (seg, GROUP * HD), 1) // HD
    total = jnp.where(lane_head == 0, square[:seg], 0.0)
    for head in range(1, GROUP):
        total = total + jnp.where(lane_head == head, square[head * seg : (head + 1) * seg], 0.0)
    return total


def one_hot_t(id_row):
    shape = (VOCAB, id_row.shape[1])
    return (id_row == lax.broadcasted_iota(jnp.int32, shape, 0)).astype(f32)


def each_chunk(count, body, state):
    if count <= 4:
        for chunk in range(count):
            state = body(chunk, state)
        return state
    return lax.fori_loop(0, count, body, state)


def two(values):
    return jnp.concatenate([values, values], 1)


def rotated_rows(one_hot, table, cosine, sine):
    plain = dot(one_hot, table)
    swapped = dot(one_hot, swap_pairs(table.astype(f32)).astype(bf16))
    return plain * two(cosine) + swapped * two(sine)


def prepare_block(first_ref, ids_ref, own_ref, q_ref, k_ref, cos_ref, sin_ref, key_ref, hot_ref):
    seg = own_ref.shape[2]
    hot_t = one_hot_t(ids_ref[0])
    hot_ref[...] = hot_t.T.astype(bf16)
    first = pl.multiple_of(first_ref[0], seg)
    own_hot_t = one_hot_t(own_ref[0])
    queries = rotated_rows(
        own_hot_t.T.astype(bf16), q_ref[...], cos_ref[pl.ds(first, seg), :], sin_ref[pl.ds(first, seg), :]
    ) * (HD ** (-0.5))
    spread = spread_heads(queries, seg).astype(bf16)
    return hot_t.astype(bf16), own_hot_t.astype(bf16), first, spread


def allowed_at(chunk, size, first, seg):
    shape = (size, GROUP * seg)
    key_at = chunk * size + lax.broadcasted_iota(jnp.int32, shape, 0)
    query_at = first + lax.broadcasted_iota(jnp.int32, shape, 1) % seg
    return key_at <= query_at


def rows_of(chunk, size):
    return pl.ds(pl.multiple_of(chunk * size, size), size)


def attend_kernel(
    first_ref, ids_ref, own_ref, q_ref, k_ref, v_ref, cos_ref, sin_ref,
    att_ref, share_ref, total_ref, key_ref, hot_ref, score_ref, hot_t_ref,
):
    seg = own_ref.shape[2]
    length = ids_ref.shape[2]
    size = min(length, 512)
    hot_t, own_hot_t, first, spread = prepare_block(
        first_ref, ids_ref, own_ref, q_ref, k_ref, cos_ref, sin_ref, key_ref, hot_ref
    )
    for part in range(length // size):
        hot_t_ref[part] = hot_t[:, part * size : (part + 1) * size]

    def scores(chunk, top):
        rows = rows_of(chunk, size)
        keys = rotated_rows(hot_ref[rows, :], k_ref[...], cos_ref[rows, :], sin_ref[rows, :]).astype(bf16)
        block = dot_nt(keys, spread)
        block = jnp.where(allowed_at(chunk, size, first, seg), block, masked_value)
        score_ref[rows, :] = block
        return jnp.maximum(top, jnp.max(block, 0, keepdims=True))

    top = each_chunk(length // size, scores, jnp.full((1, GROUP * seg), masked_value, f32))

    def shares(chunk, state):
        mass, share = state
        prob = jnp.exp(score_ref[rows_of(chunk, size), :] - top)
        return (
            mass + jnp.sum(prob, 0, keepdims=True),
            share + dot(hot_t_ref[chunk], prob.astype(bf16)),
        )

    mass, share = each_chunk(
        length // size,
        shares,
        (jnp.zeros((1, GROUP * seg), f32), jnp.zeros((VOCAB, GROUP * seg), f32)),
    )
    share = share / mass
    share_ref[0, 0] = share
    total_ref[0, 0] = top + jnp.log(mass)
    share_rows = share.T
    high = share_rows.astype(bf16)
    rest = (share_rows - high.astype(f32)).astype(bf16)
    values = v_ref[...]
    square = dot(high, values) + dot(rest, values)
    att_ref[0] = pick_heads(square, seg).astype(bf16)


def attend_back_kernel(
    first_ref, ids_ref, own_ref, q_ref, k_ref, v_ref, cos_ref, sin_ref, share_ref, total_ref, grad_ref,
    out_ref, key_ref, hot_ref, hot_t_ref,
):
    seg = own_ref.shape[2]
    length = ids_ref.shape[2]
    size = min(length, 512)
    hot_t, own_hot_t, first, spread = prepare_block(
        first_ref, ids_ref, own_ref, q_ref, k_ref, cos_ref, sin_ref, key_ref, hot_ref
    )
    for part in range(length // size):
        hot_t_ref[part] = hot_t[:, part * size : (part + 1) * size]
    share = share_ref[0, 0]
    total = total_ref[0, 0]
    grad = spread_heads(grad_ref[0].astype(f32), seg).astype(bf16)
    value_grad = dot(share.astype(bf16), grad)
    each = dot_nt(v_ref[...], grad)
    each = each - jnp.sum(each * share, 0, keepdims=True)
    high = each.astype(bf16)
    each_two = jnp.concatenate([high, (each - high.astype(f32)).astype(bf16)], 0)

    def advance(chunk, state):
        query_part, key_plain, key_swap = state
        rows = rows_of(chunk, size)
        hot = hot_ref[rows, :]
        cosine, sine = two(cos_ref[rows, :]), two(sin_ref[rows, :])
        keys = rotated_rows(hot, k_ref[...], cos_ref[rows, :], sin_ref[rows, :]).astype(bf16)
        block = dot_nt(keys, spread)
        prob = jnp.where(allowed_at(chunk, size, first, seg), jnp.exp(block - total), 0.0)
        slope = (prob * dot(jnp.concatenate([hot, hot], 1), each_two)).astype(bf16)
        query_part = query_part + dot_tn(slope, keys)
        key_part = dot(slope, spread)
        hot_t_part = hot_t_ref[chunk]
        key_plain = key_plain + dot(hot_t_part, (key_part * cosine).astype(bf16))
        key_swap = key_swap + dot(hot_t_part, (key_part * sine).astype(bf16))
        return (query_part, key_plain, key_swap)

    wide = GROUP * HD
    query_part, key_plain, key_swap = each_chunk(
        length // size,
        advance,
        (jnp.zeros((GROUP * seg, wide), f32), jnp.zeros((VOCAB, wide), f32), jnp.zeros((VOCAB, wide), f32)),
    )
    query_rows = pick_heads(query_part, seg) * (HD ** (-0.5))
    own_cos, own_sin = cos_ref[pl.ds(first, seg), :], sin_ref[pl.ds(first, seg), :]
    query_plain = dot(own_hot_t, (query_rows * two(own_cos)).astype(bf16))
    query_swap = dot(own_hot_t, (query_rows * two(own_sin)).astype(bf16))
    parts = (query_plain - swap_pairs(query_swap), key_plain - swap_pairs(key_swap), value_grad)

    @pl.when(pl.program_id(1) == 0)
    def _():
        for member in range(3):
            out_ref[member] = parts[member]

    @pl.when(pl.program_id(1) > 0)
    def _():
        for member in range(3):
            out_ref[member] = out_ref[member] + parts[member]


def attention_calls(sequences, seg, length, width):
    groups = H // GROUP
    wide = GROUP * HD
    rows = GROUP * seg
    smem = pl.BlockSpec(memory_space=pltpu.SMEM)
    by_seq = lambda extent: pl.BlockSpec((1, 1, extent), lambda g, s: (s, 0, 0))
    by_group = pl.BlockSpec((VOCAB, wide), lambda g, s: (0, g))
    turn = pl.BlockSpec((length, 2 * HD), lambda g, s: (0, 0))
    common = [smem, by_seq(length), by_seq(seg), by_group, by_group, by_group, turn, turn]
    share_spec = pl.BlockSpec((1, 1, VOCAB, rows), lambda g, s: (s, g, 0, 0))
    total_spec = pl.BlockSpec((1, 1, 1, rows), lambda g, s: (s, g, 0, 0))
    row_spec = pl.BlockSpec((1, seg, wide), lambda g, s: (s, 0, g))
    size = min(length, 512)
    scratch = [pltpu.VMEM((16, 128), bf16), pltpu.VMEM((length, VOCAB), bf16)]
    turned = pltpu.VMEM((length // size, VOCAB, size), bf16)
    params = pltpu.CompilerParams(vmem_limit_bytes=VMEM_BYTES)
    forward = pl.pallas_call(
        attend_kernel,
        grid=(groups, sequences),
        in_specs=common,
        out_specs=(row_spec, share_spec, total_spec),
        out_shape=(
            jax.ShapeDtypeStruct((sequences, seg, width), bf16),
            jax.ShapeDtypeStruct((sequences, groups, VOCAB, rows), f32),
            jax.ShapeDtypeStruct((sequences, groups, 1, rows), f32),
        ),
        scratch_shapes=scratch + [pltpu.VMEM((length, rows), f32), turned],
        compiler_params=params,
        name="attend",
    )
    backward = pl.pallas_call(
        attend_back_kernel,
        grid=(groups, sequences),
        in_specs=common + [share_spec, total_spec, row_spec],
        out_specs=pl.BlockSpec((3, VOCAB, wide), lambda g, s: (0, 0, g)),
        out_shape=jax.ShapeDtypeStruct((3, VOCAB, width), f32),
        scratch_shapes=scratch + [turned],
        compiler_params=params,
        name="attend_back",
    )
    return forward, backward


def turn_tables(length):
    half = ROT // 2
    frequency = jnp.exp(jnp.arange(half).astype(f32) * (-2.0 * math.log(10000.0) / ROT))
    angles = jnp.arange(length).astype(f32)[:, None] * frequency[None, :]
    cosine, sine = jnp.cos(angles), jnp.sin(angles)
    rest = jnp.zeros((length, HD - ROT), f32)
    cosine = jnp.concatenate([cosine, cosine, rest + 1.0], 1)
    sine = jnp.concatenate([sine, sine, rest], 1)
    return two(cosine), two(sine)


def swap_all(values, axes):
    return lax.all_to_all(values, axes, 0, 0, tiled=True)


def to_all(values, count):
    return jnp.broadcast_to(values[None], (count,) + values.shape)


def shards(
    ids, targets, flags, tags, partner,
    embedding, gains, attn_qkv, attn_out, mlp_in, mlp_out, out_head,
    first_embedding, first_gains, first_attn_qkv, first_attn_out, first_mlp_in, first_mlp_out, first_out_head,
    second_embedding, second_gains, second_attn_qkv, second_attn_out, second_mlp_in, second_mlp_out, second_out_head,
):
    masters = (embedding, gains, attn_qkv, attn_out, mlp_in, mlp_out, out_head)
    firsts = (first_embedding, first_gains, first_attn_qkv, first_attn_out, first_mlp_in, first_mlp_out, first_out_head)
    seconds = (
        second_embedding, second_gains, second_attn_qkv, second_attn_out, second_mlp_in, second_mlp_out, second_out_head,
    )
    n = lax.axis_size("blk")
    nb = lax.axis_size("batch")
    na = n * nb
    blk = lax.axis_index("blk")
    batch = lax.axis_index("batch")
    sequences, seg = ids.shape
    length = n * seg
    tokens = sequences * seg
    width = attn_out.shape[1]
    dl = attn_out.shape[0]
    fl = mlp_out.shape[0]
    hidden = mlp_in.shape[1]
    groups = H // GROUP
    total_seqs = sequences * nb

    low_embed, low_gains, low_qkv, low_attn, low_inner, low_outer, low_head = tuple(
        weight.astype(bf16) for weight in masters
    )
    w_attn = lax.all_gather(low_attn, "blk", axis=0, tiled=True)
    cosine, sine = turn_tables(length)

    embed = low_embed.astype(f32)
    gain_first = low_gains[0:1].astype(f32)
    own_mean = jnp.mean(embed, -1, keepdims=True)
    centered = embed - own_mean
    own_square = jnp.sum(centered * centered, -1, keepdims=True)
    left = jnp.concatenate([(centered * gain_first).astype(bf16), low_gains[0:1], jnp.zeros((7, dl), bf16)], 0)
    part_qkv = dot(left, low_qkv).astype(bf16).reshape(40, 3, n, dl)
    part_inner = dot(left, low_inner).astype(bf16).reshape(40, n, fl)
    stats = jnp.concatenate(
        split(own_mean, 3) + split(own_square, 3) + [jnp.zeros((VOCAB, seg - 6), bf16)], 1
    )
    stats = jnp.concatenate([stats, ids.astype(bf16), jnp.zeros((8 - sequences, seg), bf16)], 0)
    sent = jnp.concatenate(
        [
            jnp.transpose(part_qkv, (2, 0, 1, 3)).reshape(n, 40, 3 * dl),
            jnp.transpose(part_inner, (1, 0, 2)),
            to_all(stats, n),
        ],
        2,
    )
    got = swap_all(sent, "blk")
    cols = 3 * dl + fl
    got_stats = got[:, :VOCAB, cols : cols + 6].astype(f32)
    means = got_stats[:, :, 0:1] + got_stats[:, :, 1:2] + got_stats[:, :, 2:3]
    squares = got_stats[:, :, 3:4] + got_stats[:, :, 4:5] + got_stats[:, :, 5:6]
    average = jnp.mean(means, 0)
    shifts = means - average
    variance = (jnp.sum(squares, 0) + dl * jnp.sum(shifts * shifts, 0)) / width
    rstd = lax.rsqrt(variance + norm_eps)
    table = rstd * jnp.sum(
        got[:, :VOCAB, :cols].astype(f32) + shifts * got[:, VOCAB : VOCAB + 1, :cols].astype(f32), 0
    )
    id_rows = jnp.transpose(got[:, VOCAB : VOCAB + sequences, cols : cols + seg], (1, 0, 2))
    id_rows = id_rows.reshape(sequences, 1, length).astype(jnp.int32)
    unit = (embed - average) * rstd
    normed_low = (unit * gain_first).astype(bf16)
    projected_low = table[:, : 3 * dl].astype(bf16)
    own_value = projected_low[:, 2 * dl :]
    activated, gelu_back = jax.vjp(lambda whole: jax.nn.gelu(whole, approximate=True), table[:, 3 * dl :])
    activated_low = activated.astype(bf16)
    branch_part = dot(activated_low, low_outer).astype(bf16).reshape(VOCAB, n, dl)
    got = swap_all(
        jnp.concatenate([to_all(projected_low, n), jnp.transpose(branch_part, (1, 0, 2))], 2), "blk"
    )

    def whole_table(member):
        return jnp.transpose(got[:, :, member * dl : (member + 1) * dl], (1, 0, 2)).reshape(VOCAB, width)

    q_table, k_table, v_table = whole_table(0), whole_table(1), whole_table(2)
    own_mix = embed + jnp.sum(got[:, :, 3 * dl :].astype(f32), 0)
    mix_high, mix_rest = split(own_mix, 2)
    extra = jnp.concatenate([low_gains[1:2], jnp.zeros((VOCAB - 1, dl), bf16)], 0)
    got = swap_all(
        to_all(
            jnp.concatenate(
                [jnp.concatenate([mix_high, mix_rest], 1), jnp.concatenate([low_head.T, extra], 1)], 0
            ),
            n,
        ),
        "blk",
    )

    def whole_rows(first_row, rows, side):
        piece = got[:, first_row : first_row + rows, side * dl : (side + 1) * dl]
        return jnp.transpose(piece, (1, 0, 2)).reshape(rows, width)

    mix_table = jnp.concatenate([whole_rows(0, VOCAB, 0), whole_rows(0, VOCAB, 1)], 0)
    head_t = whole_rows(VOCAB, VOCAB, 0)
    gain_last = whole_rows(VOCAB, 1, 1).astype(f32)

    forward, backward = attention_calls(sequences, seg, length, width)
    first = (blk * seg).astype(jnp.int32).reshape(1)
    own_ids = ids.reshape(sequences, 1, seg)
    attended, share, total = forward(first, id_rows, own_ids, q_table, k_table, v_table, cosine, sine)

    id_onehot = (ids.reshape(tokens)[:, None] == jnp.arange(VOCAB)[None, :]).astype(bf16)
    mixed = dot(jnp.concatenate([id_onehot, id_onehot], 1), mix_table) + dot(
        attended.reshape(tokens, width), w_attn
    )
    center = mixed - jnp.mean(mixed, -1, keepdims=True)
    last_rstd = lax.rsqrt(jnp.mean(center * center, -1, keepdims=True) + norm_eps)
    last_unit = center * last_rstd
    final_low = (last_unit * gain_last).astype(bf16)
    logits = dot_nt(final_low, head_t)
    lse = jax.nn.logsumexp(logits, -1, keepdims=True)
    target_onehot = (targets.reshape(tokens)[:, None] == jnp.arange(VOCAB)[None, :]).astype(f32)
    counted = flags.reshape(tokens).astype(f32)
    picked = jnp.sum(target_onehot * (logits - lse), -1)
    seq_part = jnp.sum((counted * picked).reshape(sequences, seg), -1)
    scalars = jnp.concatenate(
        [
            seq_part,
            jnp.sum(counted)[None],
            jnp.sum(counted * lse[:, 0] * lse[:, 0])[None],
            jnp.zeros((128 - sequences - 2,), f32),
        ]
    )
    got = swap_all(to_all(scalars[None], na), both).reshape(nb, n, 128)
    got = jnp.sum(got, 1)
    ll_all = got[:, :sequences].reshape(total_seqs)
    token_count = jnp.sum(got[:, sequences])
    z_sum = jnp.sum(got[:, sequences + 1])
    partner_map = (partner[:, None] == jnp.arange(total_seqs)[None, :]).astype(f32)
    ll_partner = jnp.sum(partner_map * ll_all[None, :], 1)
    tag_values = tags.astype(f32)
    tag_partner = jnp.sum(partner_map * tag_values[None, :], 1)
    pair_gap = (ll_all - ll_partner) / length
    pair_term = pair_weight / total_seqs * jnp.sum(tag_values * pair_gap * pair_gap)
    head_term = -jnp.sum(ll_all) + z_weight * z_sum
    loss_terms = jnp.stack([head_term, token_count])
    ll_weight = (
        -1.0 / token_count
        + pair_weight / total_seqs * 2.0 * (tag_values + tag_partner) * pair_gap / length
    )
    global_ids = batch * sequences + jnp.arange(sequences)
    placing = (global_ids[:, None] == jnp.arange(total_seqs)[None, :]).astype(f32)
    row_weight = jnp.repeat(jnp.sum(placing * ll_weight[None, :], 1), seg)
    softmax_rows = jnp.exp(logits - lse)
    dlogits = counted[:, None] * (
        row_weight[:, None] * (target_onehot - softmax_rows)
        + 2.0 * z_weight / token_count * lse * softmax_rows
    )
    dlogits_low = dlogits.astype(bf16)
    dfinal = dot(dlogits_low, head_t)
    lifted = dfinal * gain_last
    dmixed = last_rstd * (
        lifted
        - jnp.mean(lifted, -1, keepdims=True)
        - last_unit * jnp.mean(lifted * last_unit, -1, keepdims=True)
    )
    dbranch_low = dmixed.astype(bf16)
    dattended_low = dot_nt(dbranch_low, w_attn).astype(bf16)

    share_rows = share.reshape(sequences, groups, VOCAB, GROUP, seg)
    share_rows = jnp.transpose(share_rows, (1, 3, 2, 0, 4)).reshape(H, VOCAB, tokens).astype(bf16)
    head_sum = dot(share_rows.reshape(H * VOCAB, tokens), dbranch_low).astype(bf16)
    if n != H:
        head_sum = jnp.repeat(head_sum.reshape(H, VOCAB, width), n // H, 0).reshape(n * VOCAB, width)
    head_sum = lax.psum_scatter(head_sum, "blk", scatter_dimension=0, tiled=True)
    head_sum = lax.psum(head_sum, "batch")
    grad_attn = dot_tn(own_value, head_sum)

    by_id = dot_tn(id_onehot, dbranch_low)
    grad_head_t = dot_tn(dlogits_low, final_low)
    grad_gain_last = jnp.sum(dfinal * last_unit, 0, keepdims=True)
    misc = jnp.concatenate([by_id, grad_head_t, grad_gain_last, jnp.zeros((7, width), f32)], 0)
    misc_size = 72 * width // na // 2
    got = swap_all(misc.astype(bf16).reshape(na, 2, misc_size), both)
    own_misc = jnp.sum(got.astype(f32), 0).astype(bf16)

    dprojected = backward(
        first, id_rows, own_ids, q_table, k_table, v_table, cosine, sine, share, total,
        dattended_low.reshape(sequences, seg, width),
    )
    dprojected = jnp.transpose(dprojected, (1, 0, 2)).reshape(VOCAB, 3 * width)
    proj_size = VOCAB * 3 * width // na // 2
    got = swap_all(
        jnp.concatenate([dprojected.astype(bf16).reshape(na, 2, proj_size), to_all(own_misc, na)], 2), both
    )
    own_proj = jnp.sum(got[:, :, :proj_size].astype(f32), 0).astype(bf16)
    misc = got[:, :, proj_size:].reshape(72, width)
    by_id = misc[:VOCAB]
    dinner = gelu_back(dot_nt(by_id, low_outer))[0].astype(bf16)
    some_rows = VOCAB // nb
    inner_rows = lax.dynamic_slice_in_dim(dinner, batch * some_rows, some_rows, 0).reshape(2, some_rows * fl // 2)
    got = swap_all(to_all(jnp.concatenate([own_proj, inner_rows], 1), na), both)
    dprojected = got[:, :, :proj_size].reshape(VOCAB, 3 * width)
    dinner = jnp.transpose(got[:, :, proj_size:].reshape(nb, n, some_rows, fl), (0, 2, 1, 3)).reshape(VOCAB, hidden)

    dnormed = dot_nt(dinner, low_inner) + dot_nt(dprojected, low_qkv)
    grad_qkv = dot_tn(normed_low, dprojected)
    grad_inner = dot_tn(normed_low, dinner)
    grad_outer = dot_tn(activated_low, by_id)
    own_misc = lax.dynamic_slice_in_dim(misc, blk * dl, dl, 1).astype(f32)
    grad_head = own_misc[VOCAB : 2 * VOCAB].T
    lifted = dnormed * gain_first
    grad_gains = jnp.concatenate([jnp.sum(dnormed * unit, 0, keepdims=True), own_misc[2 * VOCAB : 2 * VOCAB + 1]], 0)
    outer_part = own_misc[:VOCAB] + rstd * lifted
    scaled_unit = rstd * unit
    known = (grad_gains, grad_qkv, grad_attn, grad_inner, grad_outer, grad_head)
    known_square = sum(jnp.sum(gradient * gradient) for gradient in known)
    sums = jnp.concatenate(
        [
            jnp.sum(entry, -1)
            for entry in (
                lifted, lifted * unit, outer_part, outer_part * outer_part, outer_part * scaled_unit,
                scaled_unit, scaled_unit * scaled_unit,
            )
        ]
        + [known_square[None], jnp.zeros((31,), f32)]
    )
    got = jnp.sum(swap_all(to_all(sums[None], n), "blk"), 0).reshape(8, VOCAB)
    mean_one = rstd * (got[0] / width)[:, None]
    mean_two = (got[1] / width)[:, None]
    one, two_, scale_one = mean_one[:, 0], mean_two[:, 0], width
    embed_square = jnp.sum(
        got[3]
        - 2.0 * one * got[2]
        - 2.0 * two_ * got[4]
        + scale_one * one * one
        + 2.0 * one * two_ * got[5]
        + two_ * two_ * got[6]
    )
    grad_embed = outer_part - mean_one - scaled_unit * mean_two
    grad_norm = jnp.sqrt(jnp.maximum(embed_square, 0.0) + got[7, 0])
    clip_scale = clip_level / jnp.maximum(grad_norm, clip_level)
    reduced = (grad_embed,) + known
    results = []
    for member in range(7):
        results += adam_update(
            masters[member],
            firsts[member],
            seconds[member],
            reduced[member] * clip_scale,
            learn_rates[member],
            decay_flags[member],
        )
    return (loss_terms, pair_term, grad_norm) + tuple(results)


def solution(mesh):
    tokens, whole, by_column, by_row = P("batch", "blk"), P(), P(None, "blk"), P("blk", None)
    weights = (by_column, by_column) + (by_row,) * 5
    return jax.shard_map(
        shards,
        mesh=mesh,
        in_specs=(tokens,) * 3 + (whole,) * 2 + weights * 3,
        out_specs=(whole,) * 3 + tuple(spec for spec in weights for _ in range(3)),
        check_vma=False,
    )
```

```python
import functools
import math

import jax
import jax.numpy as jnp
import numpy as np
from jax import lax
from jax.experimental import pallas as pl
from jax.experimental.pallas import tpu as pltpu
from jax.sharding import PartitionSpec as P

H = 16
HD = 64
ROT = 32
NR = HD - ROT
VOCAB = 32
ADAM_STEP = 10
GROUP = 4
WROT = GROUP * ROT
CH = 512

norm_eps = 1e-05
z_weight = 0.02
pair_weight = 4.0
clip_level = 0.005
beta_one = 0.9
beta_two = 0.999
adam_eps = 1e-08
weight_decay = 0.1
learn_rates = (0.5, 0.5, 0.02, 0.2, 0.02, 0.01, 0.02)
decay_flags = (0.0, 0.0, 1.0, 1.0, 1.0, 1.0, 1.0)
masked_value = -1e30
f32 = jnp.float32
bf16 = jnp.bfloat16
both = ("batch", "blk")
VMEM_BYTES = 60 * 1024 * 1024
sds = jax.ShapeDtypeStruct


def params():
    return pltpu.CompilerParams(vmem_limit_bytes=VMEM_BYTES)


def dot(left, right):
    return jnp.dot(left, right, preferred_element_type=f32)
def dot_nt(left, right):
    return lax.dot_general(left, right, (((1,), (1,)), ((), ())), preferred_element_type=f32)

def iota(shape, axis):
    return lax.broadcasted_iota(jnp.int32, shape, axis)

def swap_pairs(values):
    width = values.shape[1]
    from_right = pltpu.roll(values, width - ROT // 2, 1)
    from_left = pltpu.roll(values, ROT // 2, 1)
    return jnp.where(iota(values.shape, 1) % ROT < ROT // 2, -from_right, from_left)

def spread_heads(rows, size):
    seg = rows.shape[0]
    shape = (GROUP * seg, GROUP * size)
    return jnp.where(iota(shape, 0) // seg == iota(shape, 1) // size, jnp.concatenate([rows] * GROUP, 0), 0.0)

def pick_heads(square, seg, size):
    lane_head = iota((seg, GROUP * size), 1) // size
    total = jnp.where(lane_head == 0, square[:seg], 0.0)
    for head in range(1, GROUP):
        total = total + jnp.where(lane_head == head, square[head * seg : (head + 1) * seg], 0.0)
    return total

def one_hot_t(id_row):
    return (id_row == iota((VOCAB, id_row.shape[1]), 0)).astype(f32)

def each_chunk(count, body, state):
    if count <= 4:
        for chunk in range(count):
            state = body(chunk, state)
        return state
    return lax.fori_loop(0, count, body, state)

def rows_of(chunk, size):
    return pl.ds(pl.multiple_of(chunk * size, size), size)

def turned(one_hot, table, cosine, sine):
    both_tables = jnp.concatenate([table, swap_pairs(table.astype(f32)).astype(bf16)], 1)
    pair = dot(one_hot, both_tables)
    return pair[:, :WROT] * cosine + pair[:, WROT:] * sine

def own_queries(own_ref, qr_ref, qn_ref, cos_ref, sin_ref, first):
    seg = own_ref.shape[2]
    parts = qr_ref.shape[1] // WROT
    own_hot = one_hot_t(own_ref[0]).T.astype(bf16)
    table = qr_ref[...]
    plain = dot(own_hot, table)
    swapped = dot(own_hot, swap_pairs(table.astype(f32)).astype(bf16))
    rest = dot(own_hot, qn_ref[...])
    cosine, sine = cos_ref[pl.ds(first, seg), :], sin_ref[pl.ds(first, seg), :]
    scale = HD ** (-0.5)
    spreads = []
    for g in range(parts):
        lanes = slice(g * WROT, (g + 1) * WROT)
        rot = (plain[:, lanes] * cosine + swapped[:, lanes] * sine) * scale
        spreads.append((spread_heads(rot, ROT).astype(bf16), spread_heads(rest[:, lanes] * scale, NR).astype(bf16)))
    return spreads

def attend_kernel(first_ref, ids_ref, own_ref, qr_ref, qn_ref, kr_ref, kn_ref, v_ref, cos_ref, sin_ref,
                  att_ref, share_ref, mass_ref, prob_ref, turn_ref, left_ref, tail_ref, score_ref, hot_ref):
    seg = own_ref.shape[2]
    length = ids_ref.shape[2]
    size = min(length, CH)
    count = length // size
    parts = att_ref.shape[2] // (GROUP * HD)
    first = pl.multiple_of(first_ref[0], seg)
    hot_t = one_hot_t(ids_ref[0])
    hot = hot_t.T
    ahead = jnp.minimum(iota((length, seg), 0) - first, seg) == iota((length, seg), 1) + 1
    tail_ref[...] = jnp.concatenate([hot, hot, ahead.astype(f32)], 1).astype(bf16)
    for part in range(count):
        hot_ref[part] = hot_t[:, part * size : (part + 1) * size].astype(bf16)
    rows = GROUP * seg
    ban = jnp.where(iota((rows, seg), 1) + 1 > iota((rows, seg), 0) % seg, masked_value, 0.0)
    spreads = own_queries(own_ref, qr_ref, qn_ref, cos_ref, sin_ref, first)
    rights, tables = [], []
    for g in range(parts):
        lanes = slice(g * WROT, (g + 1) * WROT)
        by_id = dot_nt(spreads[g][1], kn_ref[:, lanes])
        high = by_id.astype(bf16).astype(f32)
        rights.append(jnp.concatenate([spreads[g][0].astype(f32), high, by_id - high, ban], 1).astype(bf16))
        table = kr_ref[:, lanes]
        tables.append(jnp.concatenate([table, swap_pairs(table.astype(f32)).astype(bf16)], 1))

    def scores(chunk, tops):
        at = rows_of(chunk, size)
        tail = tail_ref[at, :]
        cosine, sine = cos_ref[at, :], sin_ref[at, :]
        out = []
        for g in range(parts):
            pair = dot(tail[:, :VOCAB], tables[g])
            keys = pair[:, :WROT] * cosine + pair[:, WROT:] * sine
            turn_ref[0, g, :, at] = keys.T.astype(bf16)
            block = dot_nt(jnp.concatenate([keys.astype(bf16), tail], 1), rights[g])
            score_ref[g, at, :] = block
            out.append(jnp.maximum(tops[g], jnp.max(block, 0, keepdims=True)))
        return out

    tops = each_chunk(count, scores, [jnp.full((1, rows), masked_value, f32)] * parts)

    def shares(chunk, state):
        at = rows_of(chunk, size)
        out = []
        for g in range(parts):
            mass, share = state[g]
            prob = jnp.exp(score_ref[g, at, :] - tops[g])
            prob_low = prob.astype(bf16)
            prob_ref[0, g, at, :] = prob_low
            out.append((mass + jnp.sum(prob, 0, keepdims=True), share + dot(hot_ref[chunk], prob_low)))
        return out

    state = each_chunk(count, shares, [(jnp.zeros((1, rows), f32), jnp.zeros((VOCAB, rows), f32))] * parts)
    for g in range(parts):
        mass, share = state[g]
        share = share / mass
        share_ref[0, g] = share
        mass_ref[0, g] = mass
        share_rows = share.T
        high = share_rows.astype(bf16).astype(f32)
        pair = jnp.concatenate([high, share_rows - high], 1).astype(bf16)
        values = v_ref[:, g * GROUP * HD : (g + 1) * GROUP * HD]
        square = dot(pair, jnp.concatenate([values, values], 0))
        att_ref[0, :, g * GROUP * HD : (g + 1) * GROUP * HD] = pick_heads(square, seg, HD).astype(bf16)

def attend_back_kernel(first_ref, ids_ref, own_ref, qr_ref, qn_ref, kn_ref, v_ref, cos_ref, sin_ref,
                       share_ref, mass_ref, prob_ref, turn_ref, grad_ref,
                       out_ref, hot2_ref, hot_ref):
    seg = own_ref.shape[2]
    length = ids_ref.shape[2]
    size = min(length, CH)
    count = length // size
    parts = grad_ref.shape[2] // (GROUP * HD)
    first = pl.multiple_of(first_ref[0], seg)
    hot_t = one_hot_t(ids_ref[0])
    hot = hot_t.T
    hot2_ref[...] = jnp.concatenate([hot, hot], 1).astype(bf16)
    for part in range(count):
        hot_ref[part] = hot_t[:, part * size : (part + 1) * size].astype(bf16)
    rows = GROUP * seg
    wide = GROUP * HD
    own_hot_t = one_hot_t(own_ref[0]).astype(bf16)
    own_cos, own_sin = cos_ref[pl.ds(first, seg), :], sin_ref[pl.ds(first, seg), :]
    spreads = own_queries(own_ref, qr_ref, qn_ref, cos_ref, sin_ref, first)
    eaches = []
    for g in range(parts):
        share = share_ref[0, g]
        grad = spread_heads(grad_ref[0, :, g * wide : (g + 1) * wide].astype(f32), HD).astype(bf16)
        value_grad = dot(share.astype(bf16), grad)
        out_ref[0, 4, :, g * WROT : (g + 1) * WROT] = value_grad[:, :WROT]
        out_ref[0, 5, :, g * WROT : (g + 1) * WROT] = value_grad[:, WROT:]
        each = dot_nt(v_ref[:, g * wide : (g + 1) * wide], grad)
        each = (each - jnp.sum(each * share, 0, keepdims=True)) / mass_ref[0, g]
        high = each.astype(bf16).astype(f32)
        eaches.append(jnp.concatenate([high, each - high], 0).astype(bf16))

    def advance(chunk, state):
        at = rows_of(chunk, size)
        hot2 = hot2_ref[at, :]
        cosine, sine = cos_ref[at, :], sin_ref[at, :]
        out = []
        for g in range(parts):
            query_t, by_id, key_sum = state[g]
            slope = (prob_ref[0, g, at, :].astype(f32) * dot(hot2, eaches[g])).astype(bf16)
            query_t = query_t + dot(turn_ref[0, g, :, at], slope)
            by_id = by_id + dot(hot_ref[chunk], slope)
            key_part = dot(slope, spreads[g][0])
            pair = jnp.concatenate([key_part * cosine, key_part * sine], 1).astype(bf16)
            out.append((query_t, by_id, key_sum + dot(hot_ref[chunk], pair)))
        return out

    state = each_chunk(
        count, advance,
        [(jnp.zeros((WROT, rows), f32), jnp.zeros((VOCAB, rows), f32), jnp.zeros((VOCAB, 2 * WROT), f32))] * parts)
    scale = HD ** (-0.5)
    for g in range(parts):
        lanes = slice(g * WROT, (g + 1) * WROT)
        query_t, by_id, key_sum = state[g]
        query_rows = pick_heads(query_t.T, seg, ROT) * scale
        pair = jnp.concatenate([query_rows * own_cos, query_rows * own_sin], 1).astype(bf16)
        query_sum = dot(own_hot_t, pair)
        out_ref[0, 0, :, lanes] = query_sum[:, :WROT] - swap_pairs(query_sum[:, WROT:])
        out_ref[0, 1, :, lanes] = key_sum[:, :WROT] - swap_pairs(key_sum[:, WROT:])
        rest_rows = pick_heads(dot(by_id.T.astype(bf16), kn_ref[:, lanes]), seg, NR) * scale
        out_ref[0, 2, :, lanes] = dot(own_hot_t, rest_rows.astype(bf16))
        out_ref[0, 3, :, lanes] = dot(by_id.astype(bf16), spreads[g][1])

def attention_calls(sequences, seg, length, width):
    groups = H // GROUP
    per = groups if length <= 1024 else 1
    steps = groups // per
    wide = GROUP * HD
    rows = GROUP * seg
    smem = pl.BlockSpec(memory_space=pltpu.SMEM)
    by_seq = lambda extent: pl.BlockSpec((1, 1, extent), lambda g, s: (s, 0, 0))
    half = pl.BlockSpec((VOCAB, per * WROT), lambda g, s: (0, g))
    value = pl.BlockSpec((VOCAB, per * wide), lambda g, s: (0, g))
    turn = pl.BlockSpec((length, WROT), lambda g, s: (0, 0))
    share_spec = pl.BlockSpec((1, per, VOCAB, rows), lambda g, s: (s, g, 0, 0))
    mass_spec = pl.BlockSpec((1, per, 1, rows), lambda g, s: (s, g, 0, 0))
    prob_spec = pl.BlockSpec((1, per, length, rows), lambda g, s: (s, g, 0, 0))
    turn_spec = pl.BlockSpec((1, per, WROT, length), lambda g, s: (s, g, 0, 0))
    row_spec = pl.BlockSpec((1, seg, per * wide), lambda g, s: (s, 0, g))
    size = min(length, CH)
    hots = pltpu.VMEM((length // size, VOCAB, size), bf16)
    forward = pl.pallas_call(
        attend_kernel, grid=(steps, sequences),
        in_specs=[smem, by_seq(length), by_seq(seg), half, half, half, half, value, turn, turn],
        out_specs=(row_spec, share_spec, mass_spec, prob_spec, turn_spec),
        out_shape=(sds((sequences, seg, width), bf16), sds((sequences, groups, VOCAB, rows), f32),
                   sds((sequences, groups, 1, rows), f32), sds((sequences, groups, length, rows), bf16),
                   sds((sequences, groups, WROT, length), bf16)),
        scratch_shapes=[pltpu.VMEM((8, 128), f32), pltpu.VMEM((length, WROT), bf16), pltpu.VMEM((per, length, rows), f32), hots],
        compiler_params=params(), name="attend")
    backward = pl.pallas_call(
        attend_back_kernel, grid=(steps, sequences),
        in_specs=[smem, by_seq(length), by_seq(seg), half, half, half, value, turn, turn,
                  share_spec, mass_spec, prob_spec, turn_spec, row_spec],
        out_specs=pl.BlockSpec((1, 6, VOCAB, per * WROT), lambda g, s: (s, 0, 0, g)),
        out_shape=sds((sequences, 6, VOCAB, width // 2), f32),
        scratch_shapes=[pltpu.VMEM((length, 2 * VOCAB), bf16), hots],
        compiler_params=params(), name="attend_back")
    return forward, backward

def turn_tables(length):
    half = ROT // 2
    frequency = np.exp(np.arange(half).astype(np.float32) * np.float32(-2.0 * math.log(10000.0) / ROT)).astype(np.float32)
    angles = (np.arange(length).astype(np.float32)[:, None] * frequency[None, :]).astype(np.float32)
    cosine = np.cos(angles.astype(np.float64)).astype(np.float32)
    sine = np.sin(angles.astype(np.float64)).astype(np.float32)
    return np.tile(cosine, (1, 2 * GROUP)), np.tile(sine, (1, 2 * GROUP))

def low(values):
    return lax.reduce_precision(values, 8, 7)


def three(values):
    high = values.astype(bf16).astype(f32)
    rest = values - high
    mid = rest.astype(bf16).astype(f32)
    return [high, mid, rest - mid]


def project_kernel(batch_ref, embed_ref, gains_ref, qkv_ref, inner_ref, ids_ref, out_ref):
    n, rows, lanes = out_ref.shape
    dl = embed_ref.shape[1]
    width = qkv_ref.shape[1] // 3
    hl = dl // 2
    hf = inner_ref.shape[1] // n // 2
    sequences, seg = ids_ref.shape
    embed = embed_ref[...].astype(bf16).astype(f32)
    gain = gains_ref[0:1, :].astype(bf16).astype(f32)
    mean = jnp.mean(embed, 1, keepdims=True)
    centered = embed - mean
    square = jnp.sum(centered * centered, 1, keepdims=True)
    extra = jnp.where(iota((8, dl), 0) == 0, gain, 0.0)
    left = jnp.concatenate([centered * gain, extra], 0).astype(bf16)
    qkv = dot(left, qkv_ref[...].astype(bf16))
    inner = dot(left, inner_ref[...].astype(bf16))
    stats = three(mean) + three(square)
    columns = jnp.zeros((VOCAB, lanes - 3 * hl - hf), f32)
    for place, column in enumerate(stats):
        columns = jnp.where(iota(columns.shape, 1) == place, column, columns)
    columns = jnp.concatenate([columns, jnp.zeros((8, columns.shape[1]), f32)], 0)
    ids = jnp.concatenate([ids_ref[s : s + 1, :].astype(f32) for s in range(sequences)], 1)
    if lanes > sequences * seg:
        ids = jnp.concatenate([ids, jnp.zeros((1, lanes - sequences * seg), f32)], 1)
    is_id = iota((8, lanes), 0) == 1
    second = batch_ref[0] == 1
    for k in range(n):
        pieces = []
        for member in range(3):
            start = member * width + k * dl
            pieces.append(jnp.where(second, qkv[:, start + hl : start + dl], qkv[:, start : start + hl]))
        start = k * 2 * hf
        pieces.append(jnp.where(second, inner[:, start + hf : start + 2 * hf], inner[:, start : start + hf]))
        whole = jnp.concatenate(pieces + [columns], 1)
        tail = jnp.where(is_id, ids, whole[VOCAB:])
        out_ref[k] = jnp.concatenate([whole[:VOCAB], tail], 0).astype(bf16)


def project(batch, embedding, gains, attn_qkv, mlp_in, ids, n, lanes):
    vmem = pl.BlockSpec(memory_space=pltpu.VMEM)
    return pl.pallas_call(
        project_kernel,
        in_specs=[pl.BlockSpec(memory_space=pltpu.SMEM)] + [vmem] * 5,
        out_specs=vmem,
        out_shape=sds((n, VOCAB + 8, lanes), bf16),
        compiler_params=params(),
        name="project",
    )(batch, embedding, gains, attn_qkv, mlp_in, ids)


def gelu_parts(inner):
    scale = 0.7978845608
    cube = scale * (inner + 0.044715 * inner * inner * inner)
    bent = jnp.tanh(cube)
    slope = 0.5 * (1.0 + bent) + 0.5 * inner * (1.0 - bent * bent) * scale * (1.0 + 3.0 * 0.044715 * inner * inner)
    return 0.5 * inner * (1.0 + bent), slope


def tables_kernel(batch_ref, got_ref, embed_ref, gains_ref, outer_ref, send_ref, ids_ref, act_ref, slope_ref, stat_ref):
    n, rows, lanes = got_ref.shape
    hl = embed_ref.shape[1] // 2
    hf = act_ref.shape[1]
    na = send_ref.shape[0]
    width = outer_ref.shape[1]
    cols = 3 * hl + hf
    sequences, _, length = ids_ref.shape
    seg = length // n
    means, squares = [], []
    for k in range(n):
        block = got_ref[k].astype(f32)
        stats = block[:VOCAB, cols : cols + 6]
        means.append(stats[:, 0:1] + stats[:, 1:2] + stats[:, 2:3])
        squares.append(stats[:, 3:4] + stats[:, 4:5] + stats[:, 5:6])
    average = sum(means) / n
    shifts = [mean - average for mean in means]
    variance = (sum(squares) + 2 * hl * sum(shift * shift for shift in shifts)) / width
    rstd = lax.rsqrt(variance + norm_eps)
    table = jnp.zeros((VOCAB, cols), f32)
    for k in range(n):
        block = got_ref[k].astype(f32)
        table = table + block[:VOCAB, :cols] + shifts[k] * block[VOCAB : VOCAB + 1, :cols]
        for s in range(sequences):
            ids_ref[s, :, k * seg : (k + 1) * seg] = block[VOCAB + 1 : VOCAB + 2, s * seg : (s + 1) * seg].astype(jnp.int32)
    table = table * rstd
    active, slope = gelu_parts(table[:, 3 * hl :])
    act_low = active.astype(bf16)
    act_ref[...] = act_low
    slope_ref[...] = slope
    stat_ref[...] = jnp.where(iota((VOCAB, 128), 1) == 0, average, rstd)
    first = pl.multiple_of(batch_ref[0] * hf, hf)
    outer = outer_ref[pl.ds(first, hf), :].astype(bf16)
    branch = dot(act_low, outer)
    own = table[:, : 3 * hl]
    for k in range(na):
        dest = (k % n) * 2 * hl + (k // n) * hl
        send_ref[k] = jnp.concatenate([own, branch[:, dest : dest + hl]], 1).astype(bf16)


def tables(batch, got, embedding, gains, mlp_out, na, sequences, length):
    vmem = pl.BlockSpec(memory_space=pltpu.VMEM)
    hl = embedding.shape[1] // 2
    hf = mlp_out.shape[0] // 2
    return pl.pallas_call(
        tables_kernel,
        in_specs=[pl.BlockSpec(memory_space=pltpu.SMEM)] + [vmem] * 4,
        out_specs=(vmem,) * 5,
        out_shape=(
            sds((na, VOCAB, 4 * hl), bf16),
            sds((sequences, 1, length), jnp.int32),
            sds((VOCAB, hf), bf16),
            sds((VOCAB, hf), f32),
            sds((VOCAB, 128), f32),
        ),
        compiler_params=params(),
        name="tables",
    )(batch, got, embedding, gains, mlp_out)


def spread_kernel(batch_ref, got_ref, embed_ref, gains_ref, head_ref, send_ref, qr_ref, qn_ref, kr_ref, kn_ref, v_ref):
    na, _, lanes = got_ref.shape
    hl = lanes // 4
    n = na // 2
    second = batch_ref[0] == 1

    def half(values):
        return jnp.where(second, values[:, hl:], values[:, :hl])

    mix = half(embed_ref[...].astype(bf16).astype(f32))
    for k in range(na):
        block = got_ref[k]
        mix = mix + block[:, 3 * hl :].astype(f32)
        feature = (k % n) * 2 * hl + (k // n) * hl
        v_ref[:, feature : feature + hl] = block[:, 2 * hl : 3 * hl]
        head, inside = feature // HD, feature % HD
        q_to, k_to = (qr_ref, kr_ref) if inside < ROT else (qn_ref, kn_ref)
        place = head * ROT + inside % ROT
        q_to[:, place : place + hl] = block[:, :hl]
        k_to[:, place : place + hl] = block[:, hl : 2 * hl]
    high = mix.astype(bf16).astype(f32)
    gain = half(gains_ref[1:2, :].astype(bf16).astype(f32))
    head_t = half(head_ref[...])
    whole = jnp.concatenate([high, mix - high, head_t, jnp.broadcast_to(gain, (VOCAB, hl))], 1).astype(bf16)
    for k in range(na):
        send_ref[k] = whole


def spread(batch, got, embedding, gains, out_head, width):
    vmem = pl.BlockSpec(memory_space=pltpu.VMEM)
    half = sds((VOCAB, width // 2), bf16)
    return pl.pallas_call(
        spread_kernel,
        in_specs=[pl.BlockSpec(memory_space=pltpu.SMEM)] + [vmem] * 4,
        out_specs=(vmem,) * 6,
        out_shape=(sds(got.shape, bf16), half, half, half, half, sds((VOCAB, width), bf16)),
        compiler_params=params(),
        name="spread",
    )(batch, got, embedding, gains, out_head)


def one_hot(column):
    return (column == iota((column.shape[0], VOCAB), 1).astype(f32)).astype(f32)


def column_of(ref):
    sequences, seg = ref.shape
    rows = jnp.concatenate([ref[...].astype(f32), jnp.zeros((8 - sequences, seg), f32)], 0).T
    return jnp.concatenate([rows[:, s : s + 1] for s in range(sequences)], 0)


def head_kernel(
    sequences, att_ref, attn_ref, got_ref, ids_ref, targets_ref, flags_ref,
    send_ref, unit_ref, stat_ref, logit_ref, head_ref, gain_ref, mix_ref,
):
    na, _, lanes = got_ref.shape
    hl = lanes // 4
    n = na // 2
    tokens, width = unit_ref.shape
    for k in range(na):
        block = got_ref[k]
        feature = (k % n) * 2 * hl + (k // n) * hl
        lane = slice(feature, feature + hl)
        mix_ref[:VOCAB, lane] = block[:, :hl]
        mix_ref[VOCAB:, lane] = block[:, hl : 2 * hl]
        head_ref[:, lane] = block[:, 2 * hl : 3 * hl]
        gain_ref[:, lane] = block[:8, 3 * hl :].astype(f32)
    hot = one_hot(column_of(ids_ref))
    hot = jnp.concatenate([hot, hot], 1).astype(bf16)
    mixed = dot(hot, mix_ref[...]) + dot(att_ref[...], attn_ref[...])
    center = mixed - jnp.mean(mixed, 1, keepdims=True)
    rstd = lax.rsqrt(jnp.mean(center * center, 1, keepdims=True) + norm_eps)
    unit = center * rstd
    unit_ref[...] = unit
    final = (unit * gain_ref[0:1, :]).astype(bf16)
    logits = dot_nt(final, head_ref[...])
    top = jnp.max(logits, 1, keepdims=True)
    lse = top + jnp.log(jnp.sum(jnp.exp(logits - top), 1, keepdims=True))
    logit_ref[...] = logits
    counted = column_of(flags_ref)
    picked = counted * (jnp.sum(one_hot(column_of(targets_ref)) * logits, 1, keepdims=True) - lse)
    stat_ref[...] = jnp.where(iota((tokens, 128), 1) == 0, rstd, lse)
    seg = tokens // sequences
    entries = [jnp.sum(picked[s * seg : (s + 1) * seg], 0, keepdims=True) for s in range(sequences)]
    entries += [jnp.sum(counted, 0, keepdims=True), jnp.sum(counted * lse * lse, 0, keepdims=True)]
    row = jnp.zeros((1, 128), f32)
    for place, entry in enumerate(entries):
        row = jnp.where(iota((1, 128), 1) == place, entry, row)
    for k in range(na):
        send_ref[k] = row


def head_call(sequences, attended, w_attn, got, ids, targets, flags):
    vmem = pl.BlockSpec(memory_space=pltpu.VMEM)
    tokens, width = attended.shape
    na = got.shape[0]
    return pl.pallas_call(
        functools.partial(head_kernel, sequences),
        in_specs=[vmem] * 6,
        out_specs=(vmem,) * 6,
        out_shape=(
            sds((na, 1, 128), f32),
            sds((tokens, width), f32),
            sds((tokens, 128), f32),
            sds((tokens, VOCAB), f32),
            sds((VOCAB, width), bf16),
            sds((8, width), f32),
        ),
        scratch_shapes=[pltpu.VMEM((2 * VOCAB, width), bf16)],
        compiler_params=params(),
        name="head",
    )(attended, w_attn, got, ids, targets, flags)


def back_kernel(
    place_ref, tags_ref, partner_ref, got_ref, unit_ref, stat_ref, logit_ref, head_ref, gain_ref, attn_ref,
    ids_ref, targets_ref, flags_ref, share_ref,
    loss_ref, grad_ref, misc_ref, give_ref, keep_ref, rows_ref,
):
    na = got_ref.shape[0]
    tokens, width = unit_ref.shape
    sequences = share_ref.shape[0]
    nb = 2
    n = na // nb
    total = sequences * nb
    seg = tokens // sequences
    length = n * seg
    sums = []
    for b in range(nb):
        acc = got_ref[b * n]
        for k in range(1, n):
            acc = acc + got_ref[b * n + k]
        sums.append(acc)
    likelihood = [sums[s // sequences][:, s % sequences : s % sequences + 1] for s in range(total)]
    count = sum(part[:, sequences : sequences + 1] for part in sums)
    z_sum = sum(part[:, sequences + 1 : sequences + 2] for part in sums)
    weights, pair_term = [], jnp.zeros((1, 1), f32)
    for s in range(total):
        other, other_tag = jnp.zeros((1, 1), f32), jnp.zeros((1, 1), f32)
        for t in range(total):
            chosen = partner_ref[s] == t
            other = jnp.where(chosen, likelihood[t], other)
            other_tag = jnp.where(chosen, tags_ref[t].astype(f32), other_tag)
        tag = tags_ref[s].astype(f32)
        gap = (likelihood[s] - other) / length
        pair_term = pair_term + tag * gap * gap
        weights.append(-1.0 / count + pair_weight / total * 2.0 * (tag + other_tag) * gap / length)
    pair_term = pair_weight / total * pair_term
    head_term = z_weight * z_sum - sum(likelihood)
    row = jnp.zeros((1, 128), f32)
    for at, entry in enumerate((head_term, count, pair_term)):
        row = jnp.where(iota((1, 128), 1) == at, entry, row)
    loss_ref[...] = row
    second = place_ref[0] == 1
    own = [jnp.where(second, weights[sequences + s], weights[s]) for s in range(sequences)]
    row_at = iota((tokens, 1), 0) // seg
    row_weight = jnp.zeros((tokens, 1), f32)
    for s in range(sequences):
        row_weight = jnp.where(row_at == s, own[s], row_weight)
    rstd, lse = stat_ref[:, 0:1], stat_ref[:, 1:2]
    soft = jnp.exp(logit_ref[...] - lse)
    counted = column_of(flags_ref)
    slope = counted * (
        row_weight * (one_hot(column_of(targets_ref)) - soft) + 2.0 * z_weight / count * lse * soft
    )
    slope_low = slope.astype(bf16)
    unit = unit_ref[...]
    lifted = dot(slope_low, head_ref[...]) * gain_ref[0:1, :]
    mixed = rstd * (
        lifted
        - jnp.mean(lifted, 1, keepdims=True)
        - unit * jnp.mean(lifted * unit, 1, keepdims=True)
    )
    branch = mixed.astype(bf16)
    grad_ref[...] = dot_nt(branch, attn_ref[...]).astype(bf16)
    hot_t = one_hot(column_of(ids_ref)).T.astype(bf16)
    by_id = dot(hot_t, branch)
    by_slope = dot(slope_low.astype(f32).T.astype(bf16), unit.astype(bf16))
    hl = misc_ref.shape[2] // 2
    for k in range(na):
        feature = (k % n) * 2 * hl + (k // n) * hl
        lane = slice(feature, feature + hl)
        misc_ref[k] = jnp.concatenate([by_id[:, lane], by_slope[:, lane]], 1).astype(bf16)
    order = sorted(range(n), key=lambda k: [(k >> b) & 1 for b in range(n.bit_length() - 1)])
    for at, k in enumerate(order):
        head = k * H // n
        for s in range(sequences):
            piece = share_ref[s, head // GROUP, :, (head % GROUP) * seg : (head % GROUP + 1) * seg]
            rows_ref[at * VOCAB : (at + 1) * VOCAB, s * seg : (s + 1) * seg] = piece
    half = n * VOCAB // 2
    upper = place_ref[1] == 1
    low_rows, high_rows = rows_ref[:half, :], rows_ref[half:, :]
    give_ref[...] = dot(jnp.where(upper, low_rows, high_rows).astype(bf16), branch).astype(bf16)
    keep_ref[...] = dot(jnp.where(upper, high_rows, low_rows).astype(bf16), branch).astype(bf16)


def back_call(place, tags, partner, got, unit, stat, logits, head_t, gain, w_attn, ids, targets, flags, share, n):
    vmem = pl.BlockSpec(memory_space=pltpu.VMEM)
    smem = pl.BlockSpec(memory_space=pltpu.SMEM)
    tokens, width = unit.shape
    na = got.shape[0]
    half = sds((n * VOCAB // 2, width), bf16)
    return pl.pallas_call(
        back_kernel,
        in_specs=[smem] * 3 + [vmem] * 11,
        out_specs=(vmem,) * 5,
        out_shape=(sds((1, 128), f32), sds((tokens, width), bf16), sds((na, VOCAB, 2 * width // na), bf16), half, half),
        scratch_shapes=[pltpu.VMEM((n * VOCAB, tokens), f32)],
        compiler_params=params(),
        name="back",
    )(place, tags, partner, got, unit, stat, logits, head_t, gain, w_attn, ids, targets, flags, share)


def reduce_heads(give, keep, n, nb, blk, dproj):
    got = lax.ppermute(give, "blk", [(k, k ^ 1) for k in range(n)])
    current = keep.astype(f32) + got.astype(f32)
    steps = n.bit_length() - 1
    rounds = [(1,)] + [tuple(range(at, min(at + 2, steps))) for at in range(2, steps, 2)]
    for place, bits in enumerate(rounds):
        blocks = current.reshape((1 << len(bits), -1) + current.shape[1:])

        def block(flip):
            mine = 0
            for at, bit in enumerate(bits):
                mine = 2 * mine + ((blk >> bit) ^ (flip >> at)) % 2
            return lax.dynamic_index_in_dim(blocks, mine, 0, False)

        gives = [block(flip).astype(bf16) for flip in range(1, 1 << len(bits))]
        if place == 1:
            dproj, *gives = lax.optimization_barrier((dproj, *gives))
        current = block(0)
        for flip, give in enumerate(gives, 1):
            mask = sum(((flip >> at) & 1) << bit for at, bit in enumerate(bits))
            current = current + lax.ppermute(give, "blk", [(k, k ^ mask) for k in range(n)]).astype(f32)
    for step in range(nb.bit_length() - 1):
        give = low(current)
        got = lax.ppermute(give.astype(bf16), "batch", [(k, k ^ (1 << step)) for k in range(nb)])
        current = give + got.astype(f32)
    return current.astype(bf16), dproj


def pack_kernel(proj_ref, misc_ref, send_ref, own_ref):
    na, _, lanes = send_ref.shape
    hl = lanes // 4
    n = na // 2
    parts = []
    for member in range(6):
        part = proj_ref[0, member]
        for s in range(1, proj_ref.shape[0]):
            part = part + proj_ref[s, member]
        parts.append(part)
    own = misc_ref[0].astype(f32)
    for k in range(1, na):
        own = own + misc_ref[k].astype(f32)
    own_ref[...] = own
    by_id = own[:, :hl]
    wide = GROUP * HD
    for k in range(na):
        feature = (k % n) * 2 * hl + (k // n) * hl
        head, inside = feature // HD, feature % HD
        member = 0 if inside < ROT else 2
        at = head * ROT + inside % ROT
        group, inside = feature // wide, feature % wide
        value_at = group * WROT + inside % WROT
        pieces = [
            parts[member][:, at : at + hl],
            parts[member + 1][:, at : at + hl],
            parts[4 + inside // WROT][:, value_at : value_at + hl],
            by_id,
        ]
        send_ref[k] = jnp.concatenate(pieces, 1).astype(bf16)


def pack(proj, misc):
    vmem = pl.BlockSpec(memory_space=pltpu.VMEM)
    na, _, lanes = misc.shape
    return pl.pallas_call(
        pack_kernel,
        in_specs=[vmem] * 2,
        out_specs=(vmem,) * 2,
        out_shape=(sds((na, VOCAB, 2 * lanes), bf16), sds((VOCAB, lanes), f32)),
        compiler_params=params(),
        name="pack",
    )(proj, misc)


def inner_kernel(batch_ref, got_ref, outer_ref, slope_ref, send_ref, by_id_ref):
    na, _, lanes = got_ref.shape
    hl = lanes // 4
    n = na // 2
    hf = slope_ref.shape[1]
    total = got_ref[0].astype(f32)
    for k in range(na):
        block = got_ref[k]
        if k > 0:
            total = total + block.astype(f32)
        feature = (k % n) * 2 * hl + (k // n) * hl
        by_id_ref[:, feature : feature + hl] = block[:, 3 * hl :]
    first = pl.multiple_of(batch_ref[0] * hf, hf)
    outer = outer_ref[pl.ds(first, hf), :].astype(bf16)
    slope = dot_nt(by_id_ref[...], outer) * slope_ref[...]
    pad = send_ref.shape[2] - hf - 3 * hl
    pieces = [slope, total[:, : 3 * hl]] + ([jnp.zeros((VOCAB, pad), f32)] if pad else [])
    whole = jnp.concatenate(pieces, 1).astype(bf16)
    for k in range(na):
        send_ref[k] = whole


def inner_back(batch, got, mlp_out, slope):
    vmem = pl.BlockSpec(memory_space=pltpu.VMEM)
    na, _, lanes = got.shape
    cols = slope.shape[1] + 3 * lanes // 4
    return pl.pallas_call(
        inner_kernel,
        in_specs=[pl.BlockSpec(memory_space=pltpu.SMEM)] + [vmem] * 3,
        out_specs=(vmem,) * 2,
        out_shape=(sds((na, VOCAB, -(-cols // 128) * 128), bf16), sds((VOCAB, mlp_out.shape[1]), bf16)),
        compiler_params=params(),
        name="inner_back",
    )(batch, got, mlp_out, slope)


def square_sum(values):
    return jnp.sum(jnp.sum(values * values, 0, keepdims=True), 1, keepdims=True)


def turn(values):
    return values.astype(f32).T.astype(bf16)


def owned_kernel(
    batch_ref, got_ref, by_id_ref, embed_ref, gains_ref, stat_ref, qkv_ref, inner_ref, act_ref, act_other_ref,
    value_ref, sums_ref, misc_ref, misc_other_ref, head_ref,
    send_ref, proj_ref, wide_ref, normed_ref, act_t_ref, value_t_ref, part_ref, head_grad_ref, gain_grad_ref,
):
    na = got_ref.shape[0]
    n = na // 2
    dl = embed_ref.shape[1]
    hl = dl // 2
    hf = act_ref.shape[1]
    width = n * dl
    for k in range(na):
        block = got_ref[k]
        feature = (k % n) * dl + (k // n) * hl
        wide_at = (k % n) * 2 * hf + (k // n) * hf
        wide_ref[:, wide_at : wide_at + hf] = block[:, :hf]
        for member in range(3):
            proj_ref[:, member * width + feature : member * width + feature + hl] = block[
                :, hf + member * hl : hf + (member + 1) * hl
            ]
    second = batch_ref[0] == 1

    def whole(own, other):
        return jnp.concatenate([jnp.where(second, other, own), jnp.where(second, own, other)], 1)

    proj, wide = proj_ref[...], wide_ref[...]
    average, rstd = stat_ref[:, 0:1], stat_ref[:, 1:2]
    embed = embed_ref[...].astype(bf16).astype(f32)
    gain = gains_ref[0:1, :].astype(bf16).astype(f32)
    unit = (embed - average) * rstd
    normed_t = turn((unit * gain).astype(bf16))
    normed_ref[...] = normed_t
    dnormed = dot_nt(wide, inner_ref[...].astype(bf16)) + dot_nt(proj, qkv_ref[...].astype(bf16))
    act_t = turn(whole(act_ref[...].astype(f32), act_other_ref[...].astype(f32)))
    act_t_ref[...] = act_t
    value_t = turn(value_ref[...])
    value_t_ref[...] = value_t
    known = square_sum(dot(normed_t, proj)) + square_sum(dot(normed_t, wide))
    known = known + square_sum(dot(act_t, by_id_ref[...])) + square_sum(dot(value_t, sums_ref[...]))
    own, other = misc_ref[...], misc_other_ref[...]
    by_id = whole(own[:, :hl], other[:, :hl])
    by_slope = whole(own[:, hl:], other[:, hl:])
    gain_last = gains_ref[1:2, :].astype(bf16).astype(f32)
    head_grad = by_slope * gain_last
    head_grad_ref[...] = head_grad
    head_t = head_ref[...].astype(bf16).astype(f32)
    gain_grads = jnp.concatenate(
        [jnp.sum(dnormed * unit, 0, keepdims=True), jnp.sum(head_t * by_slope, 0, keepdims=True)], 0
    )
    gain_grad_ref[...] = gain_grads
    known = known + square_sum(head_grad) + square_sum(gain_grads)
    lifted = dnormed * gain
    part = by_id + rstd * lifted
    part_ref[...] = part
    scaled = rstd * unit
    entries = (lifted, lifted * unit, part, part * part, part * scaled, scaled, scaled * scaled)
    columns = jnp.zeros((VOCAB, 128), f32)
    lane = iota((VOCAB, 128), 1)
    for at, entry in enumerate(entries):
        columns = jnp.where(lane == at, jnp.sum(entry, 1, keepdims=True), columns)
    columns = jnp.where((lane == 7) & (iota((VOCAB, 128), 0) == 0), known, columns)
    rows = jnp.concatenate([columns, jnp.zeros((128 - VOCAB, 128), f32)], 0).T[:8]
    for k in range(n):
        send_ref[k] = rows


def owned(batch, got, by_id, embedding, gains, stats, attn_qkv, mlp_in, act, act_other, value, sums, misc, misc_other, out_head):
    vmem = pl.BlockSpec(memory_space=pltpu.VMEM)
    n = got.shape[0] // 2
    dl = embedding.shape[1]
    fl = act.shape[1] * 2
    return pl.pallas_call(
        owned_kernel,
        in_specs=[pl.BlockSpec(memory_space=pltpu.SMEM)] + [vmem] * 14,
        out_specs=(vmem,) * 9,
        out_shape=(
            sds((n, 8, 128), f32),
            sds((VOCAB, attn_qkv.shape[1]), bf16),
            sds((VOCAB, mlp_in.shape[1]), bf16),
            sds((dl, VOCAB), bf16),
            sds((fl, VOCAB), bf16),
            sds((dl, VOCAB), bf16),
            sds((VOCAB, dl), f32),
            sds((VOCAB, dl), f32),
            sds((2, dl), f32),
        ),
        compiler_params=params(),
        name="owned",
    )(batch, got, by_id, embedding, gains, stats, attn_qkv, mlp_in, act, act_other, value, sums, misc, misc_other, out_head)


def adam_step(member, scale, gradient, weight, moment_one, moment_two):
    gradient = gradient * scale
    moment_one = beta_one * moment_one + (1.0 - beta_one) * gradient
    moment_two = beta_two * moment_two + (1.0 - beta_two) * gradient * gradient
    root = jnp.sqrt(moment_two * (1.0 / (1.0 - beta_two**ADAM_STEP))) + adam_eps
    rate = learn_rates[member]
    kept = 1.0 - rate * weight_decay * decay_flags[member]
    return weight * kept - (rate / (1.0 - beta_one**ADAM_STEP)) * moment_one / root, moment_one, moment_two


TILED = (2, 4, 3, 5)
SMALL = (0, 1, 6)


def tiles_of(shapes):
    rows, width = shapes[3]
    tiles = []
    for member in TILED:
        for row in range(0, shapes[member][0], rows):
            for lane in range(0, shapes[member][1], width):
                tiles.append((member, row, lane))
    return tiles


def adam_kernel(got_ref, stat_ref, part_ref, head_grad_ref, gain_grad_ref, gains_ref, embed_ref,
                proj_ref, wide_ref, by_id_ref, sums_ref, normed_ref, act_t_ref, value_t_ref, *refs):
    sources = [refs[3 * member : 3 * member + 3] for member in range(7)]
    targets = [refs[21 + 3 * member : 24 + 3 * member] for member in range(7)]
    norm_ref, buffer_ref, in_sem, out_sem = refs[42:]
    rows, width = sources[3][0].shape
    tiles = tiles_of([values[0].shape for values in sources])

    def view(ref, tile):
        _, row, lane = tile
        return ref.at[row : row + rows, lane : lane + width]

    copies = []
    for at, tile in enumerate(tiles):
        group = [
            pltpu.make_async_copy(view(sources[tile[0]][j], tile), buffer_ref.at[at, j], in_sem.at[at, j])
            for j in range(3)
        ]
        for copy in group:
            copy.start()
        copies.append(group)
    total = got_ref[0]
    for k in range(1, got_ref.shape[0]):
        total = total + got_ref[k]
    columns = jnp.concatenate([total, jnp.zeros((120, 128), f32)], 0).T[:VOCAB]
    at = [columns[:, j : j + 1] for j in range(8)]
    average, rstd = stat_ref[:, 0:1], stat_ref[:, 1:2]
    one, other = rstd * at[0] / width, at[1] / width
    square = (
        at[3]
        - 2.0 * one * at[2]
        - 2.0 * other * at[4]
        + width * one * one
        + 2.0 * one * other * at[5]
        + other * other * at[6]
    )
    square = jnp.maximum(jnp.sum(square, 0, keepdims=True), 0.0) + at[7][0:1]
    norm = jnp.sqrt(square)
    norm_ref[...] = jnp.broadcast_to(norm, norm_ref.shape)
    scale = clip_level / jnp.maximum(norm, clip_level)
    unit = (embed_ref[...].astype(bf16).astype(f32) - average) * rstd
    small = (part_ref[...] - one - rstd * unit * other, gain_grad_ref[...], head_grad_ref[...])
    for member, gradient in zip(SMALL, small):
        values = adam_step(member, scale, gradient, *(ref[...] for ref in sources[member]))
        for ref, value in zip(targets[member], values):
            ref[...] = value
    outs = []
    for at, tile in enumerate(tiles):
        member, row, lane = tile
        if member == 5:
            gradient = dot(act_t_ref[row : row + rows, :], by_id_ref[...])
        elif member == 3:
            gradient = dot(value_t_ref[...], sums_ref[...])
        else:
            factor_ref = proj_ref if member == 2 else wide_ref
            gradient = dot(normed_ref[...], factor_ref[:, lane : lane + width])
        for copy in copies[at]:
            copy.wait()
        values = adam_step(member, scale, gradient, *(buffer_ref[at, j] for j in range(3)))
        for j in range(3):
            buffer_ref[at, j] = values[j]
            copy = pltpu.make_async_copy(buffer_ref.at[at, j], view(targets[member][j], tile), out_sem.at[at, j])
            copy.start()
            outs.append(copy)
    for copy in outs:
        copy.wait()


def adam(got, stats, part, head_grad, gain_grad, gains, embedding, proj, wide, by_id, sums, normed, act_t, value_t, masters, firsts, seconds):
    vmem, anywhere = pl.BlockSpec(memory_space=pltpu.VMEM), pl.BlockSpec(memory_space=pl.ANY)
    arrays = [values[member] for member in range(7) for values in (masters, firsts, seconds)]
    triples = [anywhere if member in TILED else vmem for member in range(7) for _ in range(3)]
    count = len(tiles_of([values.shape for values in masters]))
    outs = pl.pallas_call(
        adam_kernel,
        in_specs=[vmem] * 14 + triples,
        out_specs=tuple(triples) + (vmem,),
        out_shape=tuple(sds(values.shape, f32) for values in arrays) + (sds((1, 128), f32),),
        scratch_shapes=[
            pltpu.VMEM((count, 3) + masters[3].shape, f32),
            pltpu.SemaphoreType.DMA((count, 3)),
            pltpu.SemaphoreType.DMA((count, 3)),
        ],
        compiler_params=params(),
        name="adam",
    )(got, stats, part, head_grad, gain_grad, gains, embedding, proj, wide, by_id, sums, normed, act_t, value_t, *arrays)
    return outs[:21], outs[21]


def swap_all(values, axes):
    return lax.all_to_all(values, axes, 0, 0, tiled=True)


def to_all(values, count):
    return jnp.broadcast_to(values[None], (count,) + values.shape)


def shards(
    ids, targets, flags, tags, partner,
    embedding, gains, attn_qkv, attn_out, mlp_in, mlp_out, out_head,
    first_embedding, first_gains, first_attn_qkv, first_attn_out, first_mlp_in, first_mlp_out, first_out_head,
    second_embedding, second_gains, second_attn_qkv, second_attn_out, second_mlp_in, second_mlp_out, second_out_head,
):
    masters = (embedding, gains, attn_qkv, attn_out, mlp_in, mlp_out, out_head)
    firsts = (first_embedding, first_gains, first_attn_qkv, first_attn_out, first_mlp_in, first_mlp_out, first_out_head)
    seconds = (
        second_embedding, second_gains, second_attn_qkv, second_attn_out, second_mlp_in, second_mlp_out, second_out_head,
    )
    masters, firsts, seconds = (values[:6] + (values[6].T,) for values in (masters, firsts, seconds))
    out_head = masters[6]
    n = lax.axis_size("blk")
    nb = lax.axis_size("batch")
    na = n * nb
    blk = lax.axis_index("blk")
    batch = lax.axis_index("batch")
    sequences, seg = ids.shape
    length = n * seg
    tokens = sequences * seg
    width = attn_out.shape[1]
    dl = attn_out.shape[0]
    hf = mlp_out.shape[0] // nb
    batch_at = batch.astype(jnp.int32).reshape(1)
    first = (blk * seg).astype(jnp.int32).reshape(1)
    place = jnp.stack([batch, blk % 2]).astype(jnp.int32)

    own_rows = dl // nb
    low_attn = lax.dynamic_slice_in_dim(attn_out, batch * own_rows, own_rows, 0).astype(bf16)
    w_attn = lax.all_gather(low_attn, ("blk", "batch"), axis=0, tiled=True)
    cosine, sine = turn_tables(length)
    own_ids = ids.reshape(sequences, 1, seg)

    cols = 3 * dl // nb + hf + 6
    lanes = max(-(-cols // 128) * 128, sequences * seg)
    got = swap_all(project(batch_at, embedding, gains, attn_qkv, mlp_in, ids, n, lanes), "blk")
    sent, id_rows, act_half, slope_half, stats = tables(
        batch_at, got, embedding, gains, mlp_out, na, sequences, length
    )
    sent, q_rot, q_rest, k_rot, k_rest, v_table = spread(
        batch_at, swap_all(sent, both), embedding, gains, out_head, width
    )
    got_rows = swap_all(sent, both)

    forward, backward = attention_calls(sequences, seg, length, width)
    attended, share, mass, prob, turned_keys = forward(
        first, id_rows, own_ids, q_rot, q_rest, k_rot, k_rest, v_table, cosine, sine
    )
    sent, unit, row_stats, logits, head_t, gain_last = head_call(
        sequences, attended.reshape(tokens, width), w_attn, got_rows, ids, targets, flags
    )
    losses, dattended, misc, give, keep = back_call(
        place, tags, partner, swap_all(sent, both), unit, row_stats, logits, head_t, gain_last, w_attn,
        ids, targets, flags, share, n,
    )
    got = swap_all(misc, both)
    dproj = backward(
        first, id_rows, own_ids, q_rot, q_rest, k_rest, v_table, cosine, sine, share, mass, prob, turned_keys,
        dattended.reshape(sequences, seg, width),
    )
    head_sum, dproj = reduce_heads(give, keep, n, nb, blk, dproj)
    sent, own_misc = pack(dproj, got)
    other_misc = lax.ppermute(own_misc, "batch", [(0, 1), (1, 0)])
    other_act = lax.ppermute(act_half, "batch", [(0, 1), (1, 0)])
    sent, by_id = inner_back(batch_at, swap_all(sent, both), mlp_out, slope_half)

    own_value = lax.dynamic_slice_in_dim(v_table, blk * dl, dl, 1)
    sent, proj, wide, normed, act_t, value_t, part, head_grad, gain_grad = owned(
        batch_at, swap_all(sent, both), by_id, embedding, gains, stats, attn_qkv, mlp_in, act_half, other_act,
        own_value, head_sum, own_misc, other_misc, out_head,
    )
    results, norm = adam(
        swap_all(sent, "blk"), stats, part, head_grad, gain_grad, gains, embedding, proj, wide, by_id, head_sum,
        normed, act_t, value_t, masters, firsts, seconds,
    )
    return (losses[0, :2], losses[0, 2], norm[0, 0]) + tuple(results[:18]) + tuple(x.T for x in results[18:])


def solution(mesh):
    tokens, whole, by_column, by_row = P("batch", "blk"), P(), P(None, "blk"), P("blk", None)
    weights = (by_column, by_column) + (by_row,) * 5
    return jax.shard_map(
        shards,
        mesh=mesh,
        in_specs=(tokens,) * 3 + (whole,) * 2 + weights * 3,
        out_specs=(whole,) * 3 + tuple(spec for spec in weights for _ in range(3)),
        check_vma=False,
    )
```
